32 devices in a mesh: groups: 2 (over y), edge: 16 (over z, x, core).
Axes of the slice: x: 2, y: 2, z: 4, core: 2. Of those that a mesh axis runs over, the one named last changes fastest.
Arguments:
- features: bfloat16 [64, 256, 128], P(('groups', 'edge')), parts along dimension 0, may hold values from -6 to 6
- context: bfloat16 [64, 256, 128], P(('groups', 'edge')), parts along dimension 0, may hold values from -6 to 6
- states: bfloat16 [64, 12, 256, 128], P(('groups', 'edge')), parts along dimension 0, may hold values from -3 to 3
- neighbours: int32 [64, 12], P(('groups', 'edge')), parts along dimension 0, may hold values from 0 to 31, as said below
- depths: float32 [64, 256], P(('groups', 'edge')), parts along dimension 0, may hold values from 0.5 to 2
- damping: float32 [64, 256], P(('groups', 'edge')), parts along dimension 0, may hold values from 0.5 to 32
- w_corr: bfloat16 [49, 128], replicated, may hold values from -0.875 to 0.875
- w_gates: bfloat16 [256, 256], replicated, may hold values from -0.375 to 0.375
- w_cand: bfloat16 [9, 128, 128], replicated, may hold values from -0.1875 to 0.1875
- w_motion: bfloat16 [128, 128], replicated, may hold values from -0.5 to 0.5
- w_heads: bfloat16 [2, 128], replicated, may hold values from -0.5 to 0.5
Outputs:
- new_states: bfloat16 [64, 12, 256, 128], P(('groups', 'edge')), parts along dimension 0
- new_depths: float32 [64, 256], P(('groups', 'edge')), parts along dimension 0
The draws below stay inside these ranges and needn't reach their ends.
There are 2 independent parts, one for each index of `groups`. The reference program is written for one: setup_inputs(seed, part) draws one part's arguments, and reference() takes and returns one part's arrays. A program takes and returns all parts, laid end to end along the dimension named above; an argument that names none is the same for every part. Nothing has to cross between parts.
Inputs may be any that keep to these rules, and one draw needn't show every extreme that they name: Each row neighbours[f] names 12 different keyframes, none equal to f, and every named t satisfies |t // 2 - f // 2| <= 6.
All inputs are finite; a program needn't handle non-finite values.
Results may differ from the reference program's by a relative error of at most 0.0048.
Values may be sent and summed in bfloat16 or wider, within the bound.
No kernel may reach another device: no remote copies, remote signals or barrier semaphores. Data moves between devices by JAX's collectives and lax.ppermute only.
A program may use at most 64 MiB of HBM per device.

```python
import math
import jax
import jax.numpy as jnp
from jax import lax

CHAN = 128
NEIGH = 12
REACH = 6
CORR_X = 3
CORR_Y = 3
WIDTH = 64
ROWS = 4
FR_DEV = 2
OFFS = 49
PIX = 256
FRAMES = 32


def draw_neighbours(key, part):
    window_frames = (2 * REACH + 1) * FR_DEV
    frame_ids = jnp.arange(FRAMES, dtype=jnp.int32)
    own_block = frame_ids // FR_DEV
    low_block = jnp.maximum(own_block - REACH, 0)
    high_block = jnp.minimum(own_block + REACH + 1, FRAMES // FR_DEV)
    offsets = jnp.arange(window_frames, dtype=jnp.int32)
    candidates = low_block[:, None] * FR_DEV + offsets[None, :]
    usable = (candidates < high_block[:, None] * FR_DEV) & (candidates != frame_ids[:, None])
    scores = jax.random.randint(jax.random.fold_in(key, 11), (FRAMES, window_frames), 0, 1 << 16, dtype=jnp.int32)
    scores = scores * 1024 + offsets[None, :]
    scores = jnp.where(usable, scores, scores + (1 << 28))
    ranking = jnp.argsort(scores, axis=-1, stable=True)[:, :NEIGH]
    return jnp.take_along_axis(candidates, ranking, axis=-1).astype(jnp.int32)


def block_scale(rng, extent, cuts, smallest, top_value):
    gain = 1.0
    for position, blocks in cuts:
        draws = jax.random.uniform(jax.random.fold_in(jax.random.fold_in(rng, 6), position), (blocks,), jnp.float32, smallest / len(cuts), top_value / len(cuts))
        gain = gain * jnp.repeat(jnp.exp(draws), extent[position] // blocks).reshape((-1,) + (1,) * (len(extent) - 1 - position))
    return gain


def gaussian(key, extent, scale, bound, pieces=(), kind=jnp.bfloat16):
    entries = scale * jax.random.normal(key, extent, jnp.float32)
    if pieces:
        entries = entries * block_scale(key, extent, pieces, -0.22, 0.18)
    return jnp.clip(entries, -bound, bound).astype(kind)


def setup_inputs(seed: int = 0, part: int = 0) -> dict:
    key_list = jax.random.split(jax.random.key(seed), 12)
    part_splits = jax.random.split(jax.random.fold_in(key_list[11], part), 12)
    return {
        "features": gaussian(part_splits[0], (FRAMES, PIX, CHAN), 1.0, 6.0, ((0, 16),)),
        "context": gaussian(part_splits[1], (FRAMES, PIX, CHAN), 1.0, 6.0, ((0, 16),)),
        "states": gaussian(part_splits[2], (FRAMES, NEIGH, PIX, CHAN), 0.5, 3.0, ((0, 16),)),
        "neighbours": draw_neighbours(jax.random.fold_in(jax.random.fold_in(key_list[11], part), 71), part),
        "depths": jnp.clip(0.5 + 1.5 * jax.random.uniform(part_splits[4], (FRAMES, PIX), jnp.float32) ** block_scale(part_splits[4], (FRAMES, PIX), ((0, 16),), -0.2, 0.2), 0.5, 2.0),
        "damping": jnp.clip(jnp.exp(math.log(32.0) - 4.158883 * jax.random.uniform(part_splits[5], (FRAMES, PIX), jnp.float32) ** block_scale(part_splits[5], (FRAMES, PIX), ((0, 16),), -0.2, 0.2)), 0.5, 32.0),
        "w_corr": gaussian(key_list[6], (OFFS, CHAN), OFFS ** -0.5, 0.875),
        "w_gates": gaussian(key_list[7], (2 * CHAN, 2 * CHAN), (2 * CHAN) ** -0.5, 0.375),
        "w_cand": gaussian(key_list[8], (9, CHAN, CHAN), (9 * CHAN) ** -0.5, 0.1875),
        "w_motion": gaussian(key_list[9], (CHAN, CHAN), CHAN ** -0.5, 0.5),
        "w_heads": gaussian(key_list[10], (2, CHAN), CHAN ** -0.5, 0.5),
    }


def correlate(source, target):
    pixels = source.shape[0]
    channels = source.shape[-1]
    spread = CORR_Y * WIDTH + CORR_X
    padded = jnp.pad(target, ((0, 0), (spread, spread), (0, 0))).astype(jnp.float32)
    source_wide = source.astype(jnp.float32)
    pixel_ids = lax.iota(jnp.int32, pixels)
    row_ids = pixel_ids // WIDTH
    col_ids = pixel_ids % WIDTH
    inv_root = 1.0 / math.sqrt(channels)
    columns = []
    for row_step in range(-CORR_Y, CORR_Y + 1):
        for col_step in range(-CORR_X, CORR_X + 1):
            place = spread + row_step * WIDTH + col_step
            shifted = padded[:, place:place + pixels, :]
            summed = jnp.einsum('epc,pc->ep', shifted, source_wide)
            inside = (row_ids + row_step >= 0) & (row_ids + row_step < ROWS) & (col_ids + col_step >= 0) & (col_ids + col_step < WIDTH)
            columns.append((summed * inside.astype(jnp.float32)[None] * inv_root).astype(jnp.bfloat16))
    return jnp.stack(columns, 0)

def update_block(source, ctx_rows, state_rows, target, w_corr, w_gates, w_cand, w_motion, w_heads):
    edge_count = state_rows.shape[0]
    channels = source.shape[-1]
    correlation = correlate(source, target)
    encoded = jax.nn.relu(jnp.einsum('oep,oc->epc', correlation.astype(jnp.float32), w_corr.astype(jnp.float32)))
    motion = (encoded + ctx_rows.astype(jnp.float32)[None]).astype(jnp.bfloat16).reshape(-1, channels)
    hidden = state_rows.reshape(-1, channels)
    gate_pre = jnp.dot(jnp.concatenate([hidden, motion], -1), w_gates, preferred_element_type=jnp.float32)
    update = jax.nn.sigmoid(gate_pre[:, :channels])
    reset_gate = jax.nn.sigmoid(gate_pre[:, channels:])
    reset_state = (reset_gate * hidden.astype(jnp.float32)).astype(jnp.bfloat16)
    reset_state = reset_state.reshape(edge_count, ROWS, WIDTH, channels)
    framed = jnp.pad(reset_state, ((0, 0), (1, 1), (1, 1), (0, 0)))
    conv_sum = jnp.dot(motion, w_motion, preferred_element_type=jnp.float32)
    for row_step in range(3):
        for col_step in range(3):
            tap = framed[:, row_step:row_step + ROWS, col_step:col_step + WIDTH, :].reshape(-1, channels)
            conv_sum = conv_sum + jnp.dot(tap, w_cand[3 * row_step + col_step], preferred_element_type=jnp.float32)
    candidate = jnp.tanh(conv_sum)
    new_hidden = ((1.0 - update) * hidden.astype(jnp.float32) + update * candidate).astype(jnp.bfloat16)
    head_out = jnp.dot(new_hidden, jnp.transpose(w_heads), preferred_element_type=jnp.float32)
    revision = head_out[:, 0]
    confidence = jax.nn.sigmoid(head_out[:, 1])
    return (new_hidden.reshape(edge_count, -1, channels), (confidence * revision).reshape(edge_count, -1), confidence.reshape(edge_count, -1))

def reference(features, context, states, neighbours, depths, damping, w_corr, w_gates, w_cand, w_motion, w_heads):

    def per_frame(items):
        source, ctx_rows, state_rows, index_row = items
        target = jnp.take(features, index_row, axis=0)
        return update_block(source, ctx_rows, state_rows, target, w_corr, w_gates, w_cand, w_motion, w_heads)
    new_states, pushed, confidence = lax.map(per_frame, (features, context, states, neighbours))
    flat_targets = neighbours.reshape(-1)
    weighted_sum = jax.ops.segment_sum(pushed.reshape(flat_targets.shape[0], -1), flat_targets, num_segments=FRAMES)
    weight_sum = jax.ops.segment_sum(confidence.reshape(flat_targets.shape[0], -1), flat_targets, num_segments=FRAMES)
    new_depths = depths + weighted_sum / (damping + weight_sum)
    return (new_states, new_depths)
```

```python
import functools
import math

import jax
import jax.numpy as jnp
import numpy as np
from jax import lax
from jax.experimental import pallas as pl
from jax.experimental.pallas import tpu as pltpu
from jax.sharding import PartitionSpec as P

REACH = 6
CORR_X = 3
CORR_Y = 3
WIDTH = 64
ROWS = 4
PIX = ROWS * WIDTH
EDGES_PER_STEP = 4


def passed_along(value, axis, steps):
    count = lax.axis_size(axis)
    first, last = (max(0, -steps), min(count, count - steps))
    return lax.ppermute(value, axis, [(source, source + steps) for source in range(first, last)])


def corr_picks():
    side = 2 * CORR_X + 1
    picks = np.zeros((ROWS, PIX, (2 * CORR_Y + 1) * side), np.float32)
    for y in range(ROWS):
        for y2 in range(ROWS):
            if abs(y2 - y) <= CORR_Y:
                for dx in range(-CORR_X, CORR_X + 1):
                    picks[y, (y2 * WIDTH + WIDTH - 1 - dx) % PIX, (y2 - y + CORR_Y) * side + dx + CORR_X] = 1
    return picks.reshape(ROWS * PIX, -1)


def edge_kernel(
    edges, index_ref, feat_ref, ctx_ref, state_ref, window_ref, w_corr_ref, w_gates_ref,
    w_conv_ref, w_heads_ref, new_ref, sums_ref
):
    frame = pl.program_id(0)
    part = pl.program_id(1)
    chans = feat_ref.shape[-1]
    block = edges * WIDTH

    @pl.when((frame == 0) & (part == 0))
    def _():
        sums_ref[...] = jnp.zeros_like(sums_ref)

    slots = [index_ref[frame, part * edges + g] for g in range(edges)]
    source = feat_ref[0]
    inv_root = 1.0 / math.sqrt(chans)
    xs = lax.broadcasted_iota(jnp.int32, (WIDTH, PIX), 0)
    dxs = lax.broadcasted_iota(jnp.int32, (WIDTH, PIX), 1)
    dxs = WIDTH // 2 - (dxs + 1 + WIDTH // 2) % WIDTH
    valid = ((xs + dxs >= 0) & (xs + dxs < WIDTH)).astype(jnp.float32)
    skewed = [[] for _ in range(ROWS)]
    for g in range(edges):
        scores = lax.dot_general(
            source, window_ref[slots[g]], (((1,), (1,)), ((), ())),
            preferred_element_type=jnp.float32,
        )
        for y in range(ROWS):
            rolled = pltpu.roll(
                scores[y * WIDTH : (y + 1) * WIDTH], 0, 1, stride=1, stride_axis=0
            )
            skewed[y].append((rolled * valid * inv_root).astype(jnp.bfloat16))
    motions = []
    for y in range(ROWS):
        encoded = jnp.dot(
            jnp.concatenate(skewed[y], 0), w_corr_ref[y], preferred_element_type=jnp.float32
        )
        ctx = ctx_ref[0, y * WIDTH : (y + 1) * WIDTH].astype(jnp.float32)
        ctx = jnp.concatenate([ctx] * edges, 0)
        motions.append((jnp.maximum(encoded, 0.0) + ctx).astype(jnp.bfloat16))
    motion = jnp.concatenate(motions, 0)
    hidden = jnp.concatenate(
        [
            state_ref[0, g, y * WIDTH : (y + 1) * WIDTH]
            for y in range(ROWS)
            for g in range(edges)
        ],
        0,
    )
    gate_pre = jnp.dot(
        jnp.concatenate([hidden, motion], 1), w_gates_ref[...], preferred_element_type=jnp.float32
    )
    hidden_wide = hidden.astype(jnp.float32)
    gate_tanh = jnp.tanh(0.5 * gate_pre)
    reset_state = (0.5 * hidden_wide * (1.0 + gate_tanh[:, chans:])).astype(jnp.bfloat16)
    blank = jnp.zeros((block, chans), jnp.bfloat16)
    above = jnp.concatenate([blank, reset_state[: (ROWS - 1) * block]], 0)
    below = jnp.concatenate([reset_state[block:], blank], 0)
    taps = jnp.concatenate([above, reset_state, below, motion], 1)
    conv = jnp.dot(taps, w_conv_ref[...], preferred_element_type=jnp.float32)
    total = ROWS * block
    col = lax.broadcasted_iota(jnp.int32, (total, chans), 0) % WIDTH
    conv_sum = (
        conv[:, chans : 2 * chans]
        + jnp.where(col > 0, pltpu.roll(conv[:, :chans], 1, 0), 0.0)
        + jnp.where(col < WIDTH - 1, pltpu.roll(conv[:, 2 * chans :], total - 1, 0), 0.0)
    )
    candidate = jnp.tanh(conv_sum)
    update = 0.5 + 0.5 * gate_tanh[:, :chans]
    new_hidden = (hidden_wide + update * (candidate - hidden_wide)).astype(jnp.bfloat16)
    heads = lax.dot_general(
        w_heads_ref[...], new_hidden, (((1,), (1,)), ((), ())),
        preferred_element_type=jnp.float32,
    )
    revision = heads[0:1]
    confidence = 0.5 + 0.5 * jnp.tanh(0.5 * heads[1:2])
    pushed = jnp.concatenate([confidence * revision, confidence], 0)
    for g in range(edges):
        for y in range(ROWS):
            new_ref[0, g, y * WIDTH : (y + 1) * WIDTH] = new_hidden[
                y * block + g * WIDTH : y * block + (g + 1) * WIDTH
            ]
        mine = jnp.concatenate(
            [pushed[:, y * block + g * WIDTH : y * block + (g + 1) * WIDTH] for y in range(ROWS)],
            1,
        )
        sums_ref[slots[g]] += mine


def on_device(
    features, context, states, neighbours, depths, damping,
    w_corr, w_gates, w_cand, w_motion, w_heads,
):
    frames_here, pixels, chans = features.shape
    neigh = states.shape[1]
    own_block = lax.axis_index("edge")
    mirrored = features.reshape(frames_here, ROWS, WIDTH, chans)[:, :, ::-1].reshape(features.shape)
    below_side = mirrored
    above_side = mirrored
    covered = 1
    while covered < REACH + 1:
        sending = min(covered, REACH + 1 - covered)
        tail_part = below_side[below_side.shape[0] - sending * frames_here :]
        head_part = above_side[: sending * frames_here]
        below_side = jnp.concatenate([passed_along(tail_part, "edge", covered), below_side], 0)
        above_side = jnp.concatenate([above_side, passed_along(head_part, "edge", -covered)], 0)
        covered = covered + sending
    window = jnp.concatenate([below_side, above_side[frames_here:]], 0)
    slots = window.shape[0]
    local_index = neighbours - (own_block - REACH) * frames_here

    picks = jnp.asarray(corr_picks(), jnp.bfloat16)
    w_corr_wide = jnp.dot(picks, w_corr).reshape(ROWS, PIX, chans)
    taps = w_cand.reshape(3, 3, chans, chans)
    by_col = [
        jnp.concatenate(
            [taps[0, c], taps[1, c], taps[2, c], w_motion if c == 1 else jnp.zeros_like(w_motion)],
            0,
        )
        for c in range(3)
    ]
    w_conv = jnp.concatenate(by_col, 1)
    edges = math.gcd(EDGES_PER_STEP, neigh)
    whole = pl.BlockSpec(memory_space=pltpu.VMEM)
    new_states, sums = pl.pallas_call(
        functools.partial(edge_kernel, edges),
        out_shape=(
            jax.ShapeDtypeStruct(states.shape, states.dtype),
            jax.ShapeDtypeStruct((slots, 2, pixels), jnp.float32),
        ),
        grid_spec=pltpu.PrefetchScalarGridSpec(
            num_scalar_prefetch=1,
            grid=(frames_here, neigh // edges),
            in_specs=[
                pl.BlockSpec((1, pixels, chans), lambda f, k, *_: (f, 0, 0)),
                pl.BlockSpec((1, pixels, chans), lambda f, k, *_: (f, 0, 0)),
                pl.BlockSpec((1, edges, pixels, chans), lambda f, k, *_: (f, k, 0, 0)),
                whole, whole, whole, whole, whole,
            ],
            out_specs=[
                pl.BlockSpec((1, edges, pixels, chans), lambda f, k, *_: (f, k, 0, 0)),
                whole,
            ],
        ),
        compiler_params=pltpu.CompilerParams(vmem_limit_bytes=48 * 1024 * 1024),
        name="edge_update",
    )(local_index, features, context, states, window, w_corr_wide, w_gates, w_conv, w_heads)
    partial_sums = sums.reshape(slots, 2 * pixels)
    sums = partial_sums[REACH * frames_here : (REACH + 1) * frames_here]
    for offset in range(-REACH, REACH + 1):
        if offset != 0:
            block_part = partial_sums[
                (offset + REACH) * frames_here : (offset + REACH + 1) * frames_here
            ]
            sums = sums + passed_along(block_part, "edge", offset)
    new_depths = depths + sums[:, :pixels] / (damping + sums[:, pixels:])
    return (new_states, new_depths)


def solution(mesh):
    split = P(("groups", "edge"))
    return jax.shard_map(
        on_device,
        mesh=mesh,
        in_specs=(split,) * 6 + (P(),) * 5,
        out_specs=(split, split),
        check_vma=False,
    )
```

```python
import functools
import math

import jax
import jax.numpy as jnp
import numpy as np
from jax import lax
from jax.experimental import pallas as pl
from jax.experimental.pallas import tpu as pltpu
from jax.sharding import PartitionSpec as P

REACH = 6
CORR_X = 3
CORR_Y = 3
WIDTH = 64
ROWS = 4
PIX = ROWS * WIDTH
EDGES_PER_STEP = 4


def sent(value, pairs):
    count = lax.axis_size("edge")
    return lax.ppermute(
        value, "edge", [(a, b) for a, b in pairs if 0 <= a < count and 0 <= b < count]
    )


def swapped(value, steps, odd):
    low = [i for i in range(lax.axis_size("edge")) if (i // steps) % 2 == odd]
    low = [i for i in low if i + steps < lax.axis_size("edge")]
    return sent(value, [(i, i + steps) for i in low] + [(i + steps, i) for i in low])


def gather_window(own):
    count = lax.axis_size("edge")
    beside = swapped(own, 2, 0)
    two = jnp.concatenate([own, beside], 0)
    far = sent(own, [(i, i + REACH) if i % 4 >= 2 else (i, i - REACH) for i in range(count)])
    even = swapped(two, 4, 0)
    odd = swapped(two, 4, 1)
    mine = [two, even, odd, far]
    return mine + [swapped(piece, 1, 0) for piece in mine]


def window_block(block):
    own = lax.axis_index("edge")
    group, own_group = block // 4, own // 4
    column = ((block // 2) % 2 != (own // 2) % 2).astype(jnp.int32)
    place = jnp.where(group == own_group, 0, jnp.where(group == own_group ^ 1, 2, 4)) + column
    place = jnp.where(jnp.abs(group - own_group) == 2, 6, place)
    return place + 7 * (block % 2 != own % 2).astype(jnp.int32)


def corr_picks():
    side = 2 * CORR_X + 1
    picks = np.zeros((ROWS, PIX, (2 * CORR_Y + 1) * side), np.float32)
    for y in range(ROWS):
        for y2 in range(ROWS):
            if abs(y2 - y) <= CORR_Y:
                for dx in range(-CORR_X, CORR_X + 1):
                    picks[y, (y2 * WIDTH + WIDTH - 1 - dx) % PIX, (y2 - y + CORR_Y) * side + dx + CORR_X] = 1
    return picks.reshape(ROWS * PIX, -1)


def edge_kernel(
    edges, index_ref, target_ref, feat_ref, ctx_ref, state_ref, window_ref, w_corr_ref, w_gates_ref,
    w_conv_ref, w_heads_ref, new_ref, sums_ref
):
    frame = pl.program_id(0)
    part = pl.program_id(1)
    chans = feat_ref.shape[-1]
    block = edges * WIDTH

    @pl.when((frame == 0) & (part == 0))
    def _():
        sums_ref[...] = jnp.zeros_like(sums_ref)

    slots = [index_ref[frame, part * edges + g] for g in range(edges)]
    source = feat_ref[0]
    inv_root = 1.0 / math.sqrt(chans)
    xs = lax.broadcasted_iota(jnp.int32, (WIDTH, PIX), 0)
    dxs = lax.broadcasted_iota(jnp.int32, (WIDTH, PIX), 1)
    dxs = WIDTH // 2 - (dxs + 1 + WIDTH // 2) % WIDTH
    valid = ((xs + dxs >= 0) & (xs + dxs < WIDTH)).astype(jnp.float32)
    skewed = [[] for _ in range(ROWS)]
    for g in range(edges):
        scores = lax.dot_general(
            source, window_ref[slots[g]], (((1,), (1,)), ((), ())),
            preferred_element_type=jnp.float32,
        )
        for y in range(ROWS):
            rolled = pltpu.roll(
                scores[y * WIDTH : (y + 1) * WIDTH], 0, 1, stride=1, stride_axis=0
            )
            skewed[y].append((rolled * valid * inv_root).astype(jnp.bfloat16))
    motions = []
    for y in range(ROWS):
        encoded = jnp.dot(
            jnp.concatenate(skewed[y], 0), w_corr_ref[y], preferred_element_type=jnp.float32
        )
        ctx = ctx_ref[0, y * WIDTH : (y + 1) * WIDTH].astype(jnp.float32)
        ctx = jnp.concatenate([ctx] * edges, 0)
        motions.append((jnp.maximum(encoded, 0.0) + ctx).astype(jnp.bfloat16))
    motion = jnp.concatenate(motions, 0)
    hidden = jnp.concatenate(
        [
            state_ref[0, g, y * WIDTH : (y + 1) * WIDTH]
            for y in range(ROWS)
            for g in range(edges)
        ],
        0,
    )
    gate_pre = jnp.dot(
        jnp.concatenate([hidden, motion], 1), w_gates_ref[...], preferred_element_type=jnp.float32
    )
    hidden_wide = hidden.astype(jnp.float32)
    gate_tanh = jnp.tanh(0.5 * gate_pre)
    reset_state = (0.5 * hidden_wide * (1.0 + gate_tanh[:, chans:])).astype(jnp.bfloat16)
    blank = jnp.zeros((block, chans), jnp.bfloat16)
    above = jnp.concatenate([blank, reset_state[: (ROWS - 1) * block]], 0)
    below = jnp.concatenate([reset_state[block:], blank], 0)
    taps = jnp.concatenate([above, reset_state, below, motion], 1)
    conv = jnp.dot(taps, w_conv_ref[...], preferred_element_type=jnp.float32)
    total = ROWS * block
    col = lax.broadcasted_iota(jnp.int32, (total, chans), 0) % WIDTH
    conv_sum = (
        conv[:, chans : 2 * chans]
        + jnp.where(col > 0, pltpu.roll(conv[:, :chans], 1, 0), 0.0)
        + jnp.where(col < WIDTH - 1, pltpu.roll(conv[:, 2 * chans :], total - 1, 0), 0.0)
    )
    candidate = jnp.tanh(conv_sum)
    update = 0.5 + 0.5 * gate_tanh[:, :chans]
    new_hidden = (hidden_wide + update * (candidate - hidden_wide)).astype(jnp.bfloat16)
    heads = lax.dot_general(
        w_heads_ref[...], new_hidden, (((1,), (1,)), ((), ())),
        preferred_element_type=jnp.float32,
    )
    revision = heads[0:1]
    confidence = 0.5 + 0.5 * jnp.tanh(0.5 * heads[1:2])
    pushed = jnp.concatenate([confidence * revision, confidence], 0)
    for g in range(edges):
        for y in range(ROWS):
            new_ref[0, g, y * WIDTH : (y + 1) * WIDTH] = new_hidden[
                y * block + g * WIDTH : y * block + (g + 1) * WIDTH
            ]
        mine = jnp.concatenate(
            [pushed[:, y * block + g * WIDTH : y * block + (g + 1) * WIDTH] for y in range(ROWS)],
            1,
        )
        sums_ref[target_ref[frame, part * edges + g]] += mine


def on_device(
    features, context, states, neighbours, depths, damping,
    w_corr, w_gates, w_cand, w_motion, w_heads,
):
    frames_here, pixels, chans = features.shape
    neigh = states.shape[1]
    mirrored = features.reshape(frames_here, ROWS, WIDTH, chans)[:, :, ::-1].reshape(features.shape)
    pieces = gather_window(mirrored)
    window = jnp.concatenate(pieces, 0)
    blocks = neighbours // frames_here
    local_index = window_block(blocks) * frames_here + neighbours % frames_here
    frames_all = lax.axis_size("edge") * frames_here

    picks = jnp.asarray(corr_picks(), jnp.bfloat16)
    w_corr_wide = jnp.dot(picks, w_corr).reshape(ROWS, PIX, chans)
    taps = w_cand.reshape(3, 3, chans, chans)
    by_col = [
        jnp.concatenate(
            [taps[0, c], taps[1, c], taps[2, c], w_motion if c == 1 else jnp.zeros_like(w_motion)],
            0,
        )
        for c in range(3)
    ]
    w_conv = jnp.concatenate(by_col, 1)
    edges = math.gcd(EDGES_PER_STEP, neigh)
    whole = pl.BlockSpec(memory_space=pltpu.VMEM)
    new_states, sums = pl.pallas_call(
        functools.partial(edge_kernel, edges),
        out_shape=(
            jax.ShapeDtypeStruct(states.shape, states.dtype),
            jax.ShapeDtypeStruct((frames_all, 2, pixels), jnp.float32),
        ),
        grid_spec=pltpu.PrefetchScalarGridSpec(
            num_scalar_prefetch=2,
            grid=(frames_here, neigh // edges),
            in_specs=[
                pl.BlockSpec((1, pixels, chans), lambda f, k, *_: (f, 0, 0)),
                pl.BlockSpec((1, pixels, chans), lambda f, k, *_: (f, 0, 0)),
                pl.BlockSpec((1, edges, pixels, chans), lambda f, k, *_: (f, k, 0, 0)),
                whole, whole, whole, whole, whole,
            ],
            out_specs=[
                pl.BlockSpec((1, edges, pixels, chans), lambda f, k, *_: (f, k, 0, 0)),
                whole,
            ],
        ),
        compiler_params=pltpu.CompilerParams(vmem_limit_bytes=48 * 1024 * 1024),
        name="edge_update",
    )(local_index, neighbours, features, context, states, window, w_corr_wide, w_gates, w_conv, w_heads)
    sums = sums.reshape(-1, frames_here, 2, pixels)
    arrived = lax.all_to_all(sums, "edge", 0, 0, tiled=True)
    sums = jnp.sum(arrived, 0)
    new_depths = depths + sums[:, 0] / (damping + sums[:, 1])
    return (new_states, new_depths)


def solution(mesh):
    split = P(("groups", "edge"))
    return jax.shard_map(
        on_device,
        mesh=mesh,
        in_specs=(split,) * 6 + (P(),) * 5,
        out_specs=(split, split),
        check_vma=False,
    )
```

```python
import functools
import math

import jax
import jax.numpy as jnp
import numpy as np
from jax import lax
from jax.experimental import pallas as pl
from jax.experimental.pallas import tpu as pltpu
from jax.sharding import PartitionSpec as P

REACH = 6
CORR_X = 3
CORR_Y = 3
WIDTH = 64
ROWS = 4
PIX = ROWS * WIDTH


def sent(value, pairs):
    count = lax.axis_size("edge")
    return lax.ppermute(
        value, "edge", [(a, b) for a, b in pairs if 0 <= a < count and 0 <= b < count]
    )


def swapped(value, steps, odd):
    low = [i for i in range(lax.axis_size("edge")) if (i // steps) % 2 == odd]
    low = [i for i in low if i + steps < lax.axis_size("edge")]
    return sent(value, [(i, i + steps) for i in low] + [(i + steps, i) for i in low])


def gather_window(own):
    count = lax.axis_size("edge")
    beside = swapped(own, 2, 0)
    two = jnp.concatenate([own, beside], 0)
    far = sent(own, [(i, i + REACH) if i % 4 >= 2 else (i, i - REACH) for i in range(count)])
    even = swapped(two, 4, 0)
    odd = swapped(two, 4, 1)
    mine = [two, even, odd, far]
    return mine + [swapped(piece, 1, 0) for piece in mine]


def window_block(block):
    own = lax.axis_index("edge")
    group, own_group = block // 4, own // 4
    column = ((block // 2) % 2 != (own // 2) % 2).astype(jnp.int32)
    place = jnp.where(group == own_group, 0, jnp.where(group == own_group ^ 1, 2, 4)) + column
    place = jnp.where(jnp.abs(group - own_group) == 2, 6, place)
    return place + 7 * (block % 2 != own % 2).astype(jnp.int32)


def corr_weights(w_corr):
    side = 2 * CORR_X + 1
    picks = np.zeros((ROWS, 2, PIX, (2 * CORR_Y + 1) * side), np.float32)
    for y in range(ROWS):
        for y2 in range(ROWS):
            for dx in range(-CORR_X, CORR_X + 1):
                if abs(y2 - y) <= CORR_Y:
                    for half in range(2):
                        lane = y2 * WIDTH + WIDTH - 1 - dx + half * (WIDTH // 2)
                        offset = (y2 - y + CORR_Y) * side + dx + CORR_X
                        picks[y, half, lane % PIX, offset] = 1
    picks = jnp.asarray(picks.reshape(-1, picks.shape[-1]), jnp.bfloat16)
    wide = jnp.dot(picks, w_corr).reshape(ROWS, 2, PIX, -1)
    return jnp.concatenate([wide[:, 0], wide[:, 1]], -1)


def conv_inputs(pair):
    return [r for r in range(2 * pair - 1, 2 * pair + 3) if 0 <= r < ROWS]


def conv_weights(w_cand, w_motion):
    blank = jnp.zeros_like(w_motion)
    pairs = []
    for pair in range(ROWS // 2):
        rows = []
        for dx in range(3):
            for r in conv_inputs(pair):
                rows.append(
                    jnp.concatenate(
                        [
                            w_cand[3 * (r - y + 1) + dx] if abs(r - y) <= 1 else blank
                            for y in (2 * pair, 2 * pair + 1)
                        ],
                        1,
                    )
                )
        rows.append(jnp.concatenate([w_motion, blank], 1))
        rows.append(jnp.concatenate([blank, w_motion], 1))
        pairs.append(jnp.concatenate(rows, 0))
    return jnp.stack(pairs)


def edge_kernel(
    batch, index_ref, target_ref, feat_ref, ctx_ref, state_ref, window_ref, w_corr_ref,
    w_gates_ref, w_conv_ref, w_heads_ref, new_ref, sums_ref, held_ref, sem
):
    chans = feat_ref.shape[-1]
    edges = state_ref.shape[0]
    neigh = edges // feat_ref.shape[0]
    narrow = jnp.bfloat16
    sums_ref[...] = jnp.zeros_like(sums_ref)
    inv_root = 1.0 / math.sqrt(chans)
    xs = lax.broadcasted_iota(jnp.int32, (WIDTH, PIX), 0)
    lanes = lax.broadcasted_iota(jnp.int32, (WIDTH, PIX), 1)
    scales = []
    for half in range(2):
        dxs = WIDTH // 2 - (lanes + 1 + WIDTH // 2 * (1 - half)) % WIDTH
        used = (jnp.abs(dxs) <= CORR_X) & (xs + dxs >= 0) & (xs + dxs < WIDTH)
        scales.append(jnp.where(used, inv_root, 0.0).astype(jnp.float32))
    cols = lax.broadcasted_iota(jnp.int32, (WIDTH, chans), 0)
    has_left = jnp.concatenate([cols > 0] * batch, 0)
    has_right = jnp.concatenate([cols < WIDTH - 1] * batch, 0)
    length = batch * WIDTH
    half_batch = batch // 2
    copies = []
    for start in range(0, edges, batch):
        these = list(range(start, start + batch))
        scores = [
            lax.dot_general(
                feat_ref[e // neigh], window_ref[index_ref[e // neigh, e % neigh]],
                (((1,), (1,)), ((), ())), preferred_element_type=jnp.float32,
            )
            for e in these
        ]
        motion, hidden, update_tanh, reset = [], [], [], []
        for y in range(ROWS):
            row = slice(y * WIDTH, (y + 1) * WIDTH)
            both = []
            for i in range(half_batch):
                one = pltpu.roll(scores[i][row], 0, 1, stride=1, stride_axis=0)
                two = pltpu.roll(
                    scores[i + half_batch][row], WIDTH // 2, 1, stride=1, stride_axis=0
                )
                both.append((one * scales[0] + two * scales[1]).astype(narrow))
            encoded = jnp.dot(
                jnp.concatenate(both, 0), w_corr_ref[y], preferred_element_type=jnp.float32
            )
            encoded = jnp.concatenate([encoded[:, :chans], encoded[:, chans:]], 0)
            ctx = jnp.concatenate([ctx_ref[e // neigh, row] for e in these], 0)
            motion.append((jnp.maximum(encoded, 0.0) + ctx.astype(jnp.float32)).astype(narrow))
            hidden.append(jnp.concatenate([state_ref[e, row] for e in these], 0))
        for y in range(ROWS):
            gates = jnp.tanh(
                jnp.dot(
                    jnp.concatenate([hidden[y], motion[y]], 1), w_gates_ref[...],
                    preferred_element_type=jnp.float32,
                )
            )
            half_hidden = 0.5 * hidden[y].astype(jnp.float32)
            update_tanh.append(gates[:, :chans])
            reset.append(half_hidden + half_hidden * gates[:, chans:])
        left = [jnp.where(has_left, pltpu.roll(r, 1, 0), 0.0).astype(narrow) for r in reset]
        right = [
            jnp.where(has_right, pltpu.roll(r, length - 1, 0), 0.0).astype(narrow) for r in reset
        ]
        centre = [r.astype(narrow) for r in reset]
        conv = []
        for pair in range(ROWS // 2):
            taps = [side[r] for side in (left, centre, right) for r in conv_inputs(pair)]
            taps = jnp.concatenate(taps + motion[2 * pair : 2 * pair + 2], 1)
            out = jnp.dot(taps, w_conv_ref[pair], preferred_element_type=jnp.float32)
            conv += [out[:, :chans], out[:, chans:]]
        new_hidden = []
        for y in range(ROWS):
            wide = hidden[y].astype(jnp.float32)
            update = 0.5 + 0.5 * update_tanh[y]
            new_hidden.append((wide + update * (jnp.tanh(conv[y]) - wide)).astype(narrow))
        for i, e in enumerate(these):
            mine = jnp.concatenate([n[i * WIDTH : (i + 1) * WIDTH] for n in new_hidden], 0)
            held_ref[e] = mine
            heads = lax.dot_general(
                w_heads_ref[...], mine, (((1,), (1,)), ((), ())),
                preferred_element_type=jnp.float32,
            )
            confidence = 0.5 + 0.5 * jnp.tanh(0.5 * heads[1:2])
            sums_ref[target_ref[e // neigh, e % neigh]] += jnp.concatenate(
                [confidence * heads[0:1], confidence], 0
            )
        copies.append(
            pltpu.make_async_copy(
                held_ref.at[pl.ds(start, batch)], new_ref.at[pl.ds(start, batch)],
                sem.at[start // batch],
            )
        )
        copies[-1].start()
    for copy in copies:
        copy.wait()


def on_device(
    features, context, states, neighbours, depths, damping,
    w_corr, w_gates, w_cand, w_motion, w_heads,
):
    frames_here, pixels, chans = features.shape
    edges = frames_here * states.shape[1]
    mirrored = features.reshape(frames_here, ROWS, WIDTH, chans)[:, :, ::-1].reshape(features.shape)
    window = jnp.concatenate(gather_window(mirrored), 0)
    blocks = neighbours // frames_here
    local_index = window_block(blocks) * frames_here + neighbours % frames_here
    frames_all = lax.axis_size("edge") * frames_here
    batch = 12
    vmem = pl.BlockSpec(memory_space=pltpu.VMEM)
    smem = pl.BlockSpec(memory_space=pltpu.SMEM)
    new_states, sums = pl.pallas_call(
        functools.partial(edge_kernel, batch),
        out_shape=(
            jax.ShapeDtypeStruct((edges, pixels, chans), states.dtype),
            jax.ShapeDtypeStruct((frames_all, 2, pixels), jnp.float32),
        ),
        in_specs=[smem, smem] + [vmem] * 8,
        out_specs=[pl.BlockSpec(memory_space=pl.ANY), vmem],
        scratch_shapes=[
            pltpu.VMEM((edges, pixels, chans), states.dtype),
            pltpu.SemaphoreType.DMA((edges // batch,)),
        ],
        compiler_params=pltpu.CompilerParams(vmem_limit_bytes=32 * 1024 * 1024),
        name="edge_update",
    )(
        local_index, neighbours, features, context, states.reshape(edges, pixels, chans),
        window, corr_weights(w_corr), w_gates * jnp.bfloat16(0.5),
        conv_weights(w_cand, w_motion), w_heads,
    )
    new_states = new_states.reshape(states.shape)
    sums = sums.reshape(-1, frames_here, 2, pixels)
    sums = jnp.sum(lax.all_to_all(sums, "edge", 0, 0, tiled=True), 0)
    new_depths = depths + sums[:, 0] / (damping + sums[:, 1])
    return (new_states, new_depths)


def solution(mesh):
    split = P(("groups", "edge"))
    return jax.shard_map(
        on_device,
        mesh=mesh,
        in_specs=(split,) * 6 + (P(),) * 5,
        out_specs=(split, split),
        check_vma=False,
    )
```

```python
import functools
import math

import jax
import jax.numpy as jnp
import numpy as np
from jax import lax
from jax.experimental import pallas as pl
from jax.experimental.pallas import tpu as pltpu
from jax.sharding import PartitionSpec as P

REACH = 6
CORR_X = 3
CORR_Y = 3
WIDTH = 64
ROWS = 4
SHARE = 2
PIX = ROWS * WIDTH


def sent(value, pairs):
    count = lax.axis_size("edge")
    return lax.ppermute(
        value, "edge", [(a, b) for a, b in pairs if 0 <= a < count and 0 <= b < count]
    )


def swapped(value, steps, odd):
    low = [i for i in range(lax.axis_size("edge")) if (i // steps) % 2 == odd]
    low = [i for i in low if i + steps < lax.axis_size("edge")]
    return sent(value, [(i, i + steps) for i in low] + [(i + steps, i) for i in low])


def gather_window(own):
    count = lax.axis_size("edge")
    beside = swapped(own, 2, 0)
    two = jnp.concatenate([own, beside], 0)
    step = [REACH, 8]
    far = sent(own, [(i, i + step[i % 2] * (1 if i % 4 >= 2 else -1)) for i in range(count)])
    far = sent(far, [(i, i ^ 2 if i % 2 else i) for i in range(count)])
    even = swapped(two, 4, 0)
    odd = swapped(two, 4, 1)
    mine = [two, even, odd, far]
    return mine + [swapped(piece, 1, 0) for piece in mine]


def window_block(block):
    own = lax.axis_index("edge")
    group, own_group = block // 4, own // 4
    column = ((block // 2) % 2 != (own // 2) % 2).astype(jnp.int32)
    place = jnp.where(group == own_group, 0, jnp.where(group == own_group ^ 1, 2, 4)) + column
    place = jnp.where(jnp.abs(group - own_group) == 2, 6, place)
    return place + 7 * (block % 2 != own % 2).astype(jnp.int32)


def corr_weights(w_corr):
    side = 2 * CORR_X + 1
    picks = np.zeros((ROWS, SHARE, PIX, (2 * CORR_Y + 1) * side), np.float32)
    for y in range(ROWS):
        for y2 in range(ROWS):
            for dx in range(-CORR_X, CORR_X + 1):
                if abs(y2 - y) <= CORR_Y:
                    for k in range(SHARE):
                        lane = y2 * WIDTH + WIDTH - 1 - dx + k * (WIDTH // SHARE)
                        offset = (y2 - y + CORR_Y) * side + dx + CORR_X
                        picks[y, k, lane % PIX, offset] = 1
    picks = jnp.asarray(picks.reshape(-1, picks.shape[-1]), jnp.bfloat16)
    wide = jnp.dot(picks, w_corr).reshape(ROWS, SHARE, PIX, -1)
    return jnp.concatenate([wide[:, k] for k in range(SHARE)], -1)


def conv_inputs(pair):
    return [r for r in range(2 * pair - 1, 2 * pair + 3) if 0 <= r < ROWS]


def conv_weights(w_cand, w_motion):
    blank = jnp.zeros_like(w_motion)
    pairs = []
    for pair in range(ROWS // 2):
        rows = []
        for dx in range(3):
            for r in conv_inputs(pair):
                rows.append(
                    jnp.concatenate(
                        [
                            w_cand[3 * (r - y + 1) + dx] if abs(r - y) <= 1 else blank
                            for y in (2 * pair, 2 * pair + 1)
                        ],
                        1,
                    )
                )
        rows.append(jnp.concatenate([w_motion, blank], 1))
        rows.append(jnp.concatenate([blank, w_motion], 1))
        pairs.append(jnp.concatenate(rows, 0))
    return jnp.stack(pairs)


def edge_kernel(
    batch, index_ref, target_ref, feat_ref, ctx_ref, state_ref, window_ref, w_corr_ref,
    w_gates_ref, w_conv_ref, w_heads_ref, new_ref, sums_ref, held_ref, sem
):
    chans = feat_ref.shape[-1]
    edges = state_ref.shape[0]
    neigh = edges // feat_ref.shape[0]
    narrow = jnp.bfloat16
    sums_ref[...] = jnp.zeros_like(sums_ref)
    inv_root = 1.0 / math.sqrt(chans)
    xs = lax.broadcasted_iota(jnp.int32, (WIDTH, PIX), 0)
    lanes = lax.broadcasted_iota(jnp.int32, (WIDTH, PIX), 1)
    scales = []
    for k in range(SHARE):
        target = WIDTH - 1 - (lanes + PIX - k * (WIDTH // SHARE)) % WIDTH
        scales.append(jnp.where(jnp.abs(target - xs) <= CORR_X, inv_root, 0.0).astype(jnp.float32))
    cols = lax.broadcasted_iota(jnp.int32, (WIDTH, chans), 0)
    has_left = jnp.concatenate([cols > 0] * batch, 0)
    has_right = jnp.concatenate([cols < WIDTH - 1] * batch, 0)
    length = batch * WIDTH
    quarter = batch // SHARE
    copies = []
    for start in range(0, edges, batch):
        these = list(range(start, start + batch))
        scores = []
        for i, e in enumerate(these):
            target = window_ref.at[index_ref[e // neigh, e % neigh]]
            turn = i // quarter * (WIDTH // SHARE)
            target = [target[PIX - turn :], target[: PIX - turn]] if turn else [target[...]]
            scores.append(
                lax.dot_general(
                    feat_ref[e // neigh], jnp.concatenate(target, 0),
                    (((1,), (1,)), ((), ())), preferred_element_type=jnp.float32,
                )
            )
        motion, hidden, update_tanh, reset = [], [], [], []
        for y in range(ROWS):
            row = slice(y * WIDTH, (y + 1) * WIDTH)
            shared = []
            for i in range(quarter):
                bands = sum(scores[i + k * quarter][row] * scales[k] for k in range(SHARE))
                shared.append(pltpu.roll(bands, 0, 1, stride=1, stride_axis=0).astype(narrow))
            encoded = jnp.dot(
                jnp.concatenate(shared, 0), w_corr_ref[y], preferred_element_type=jnp.float32
            )
            encoded = jnp.concatenate(
                [encoded[:, k * chans : (k + 1) * chans] for k in range(SHARE)], 0
            )
            ctx = jnp.concatenate([ctx_ref[e // neigh, row] for e in these], 0)
            motion.append((jnp.maximum(encoded, 0.0) + ctx.astype(jnp.float32)).astype(narrow))
            hidden.append(jnp.concatenate([state_ref[e, row] for e in these], 0))
        for y in range(ROWS):
            gates = jnp.tanh(
                jnp.dot(
                    jnp.concatenate([hidden[y], motion[y]], 1), w_gates_ref[...],
                    preferred_element_type=jnp.float32,
                )
            )
            half_hidden = 0.5 * hidden[y].astype(jnp.float32)
            update_tanh.append(gates[:, :chans])
            reset.append(half_hidden + half_hidden * gates[:, chans:])
        left = [jnp.where(has_left, pltpu.roll(r, 1, 0), 0.0).astype(narrow) for r in reset]
        right = [
            jnp.where(has_right, pltpu.roll(r, length - 1, 0), 0.0).astype(narrow) for r in reset
        ]
        centre = [r.astype(narrow) for r in reset]
        done = []
        for pair in range(ROWS // 2):
            taps = [side[r] for side in (left, centre, right) for r in conv_inputs(pair)]
            taps = jnp.concatenate(taps + motion[2 * pair : 2 * pair + 2], 1)
            conv = jnp.dot(taps, w_conv_ref[pair], preferred_element_type=jnp.float32)
            for part in range(2):
                y = 2 * pair + part
                wide = hidden[y].astype(jnp.float32)
                update = 0.5 + 0.5 * update_tanh[y]
                candidate = jnp.tanh(conv[:, part * chans : (part + 1) * chans])
                done.append((wide + update * (candidate - wide)).astype(narrow))
                for i, e in enumerate(these):
                    held_ref[e, y * WIDTH : (y + 1) * WIDTH] = done[y][i * WIDTH : (i + 1) * WIDTH]
            place = (pl.ds(start, batch), pl.ds(2 * pair * WIDTH, 2 * WIDTH))
            copies.append(
                pltpu.make_async_copy(
                    held_ref.at[place], new_ref.at[place], sem.at[start // batch, pair]
                )
            )
            copies[-1].start()
        for i, e in enumerate(these):
            mine = jnp.concatenate([n[i * WIDTH : (i + 1) * WIDTH] for n in done], 0)
            heads = lax.dot_general(
                w_heads_ref[...], mine, (((1,), (1,)), ((), ())),
                preferred_element_type=jnp.float32,
            )
            confidence = 0.5 + 0.5 * jnp.tanh(0.5 * heads[1:2])
            sums_ref[target_ref[e // neigh, e % neigh]] += jnp.concatenate(
                [confidence * heads[0:1], confidence], 0
            )
    for copy in copies:
        copy.wait()


def on_device(
    features, context, states, neighbours, depths, damping,
    w_corr, w_gates, w_cand, w_motion, w_heads,
):
    frames_here, pixels, chans = features.shape
    edges = frames_here * states.shape[1]
    mirrored = features.reshape(frames_here, ROWS, WIDTH, chans)[:, :, ::-1].reshape(features.shape)
    window = jnp.concatenate(gather_window(mirrored), 0)
    blocks = neighbours // frames_here
    local_index = window_block(blocks) * frames_here + neighbours % frames_here
    frames_all = lax.axis_size("edge") * frames_here
    batch = 12
    vmem = pl.BlockSpec(memory_space=pltpu.VMEM)
    smem = pl.BlockSpec(memory_space=pltpu.SMEM)
    new_states, sums = pl.pallas_call(
        functools.partial(edge_kernel, batch),
        out_shape=(
            jax.ShapeDtypeStruct((edges, pixels, chans), states.dtype),
            jax.ShapeDtypeStruct((frames_all, 2, pixels), jnp.float32),
        ),
        in_specs=[smem, smem] + [vmem] * 8,
        out_specs=[pl.BlockSpec(memory_space=pl.ANY), vmem],
        scratch_shapes=[
            pltpu.VMEM((edges, pixels, chans), states.dtype),
            pltpu.SemaphoreType.DMA((edges // batch, ROWS // 2)),
        ],
        compiler_params=pltpu.CompilerParams(vmem_limit_bytes=32 * 1024 * 1024),
        name="edge_update",
    )(
        local_index, neighbours, features, context, states.reshape(edges, pixels, chans),
        window, corr_weights(w_corr), w_gates * jnp.bfloat16(0.5),
        conv_weights(w_cand, w_motion), w_heads,
    )
    new_states = new_states.reshape(states.shape)
    sums = sums.reshape(-1, frames_here, 2, pixels)
    sums = jnp.sum(lax.all_to_all(sums, "edge", 0, 0, tiled=True), 0)
    new_depths = depths + sums[:, 0] / (damping + sums[:, 1])
    return (new_states, new_depths)


def solution(mesh):
    split = P(("groups", "edge"))
    return jax.shard_map(
        on_device,
        mesh=mesh,
        in_specs=(split,) * 6 + (P(),) * 5,
        out_specs=(split, split),
        check_vma=False,
    )
```

```python
import functools
import math

import jax
import jax.numpy as jnp
import numpy as np
from jax import lax
from jax.experimental import pallas as pl
from jax.experimental.pallas import tpu as pltpu
from jax.sharding import PartitionSpec as P

REACH = 6
CORR_X = 3
CORR_Y = 3
WIDTH = 64
ROWS = 4
SHARE = 4
PIX = ROWS * WIDTH


def sent(value, pairs):
    count = lax.axis_size("edge")
    return lax.ppermute(
        value, "edge", [(a, b) for a, b in pairs if 0 <= a < count and 0 <= b < count]
    )


def swapped(value, steps, odd):
    low = [i for i in range(lax.axis_size("edge")) if (i // steps) % 2 == odd]
    low = [i for i in low if i + steps < lax.axis_size("edge")]
    return sent(value, [(i, i + steps) for i in low] + [(i + steps, i) for i in low])


def gather_window(own):
    count = lax.axis_size("edge")
    beside = swapped(own, 2, 0)
    two = jnp.concatenate([own, beside], 0)
    step = [REACH, 8]
    far = sent(own, [(i, i + step[i % 2] * (1 if i % 4 >= 2 else -1)) for i in range(count)])
    far = sent(far, [(i, i ^ 2 if i % 2 else i) for i in range(count)])
    even = swapped(two, 4, 0)
    odd = swapped(two, 4, 1)
    mine = [two, even, odd, far]
    return mine + [swapped(piece, 1, 0) for piece in mine]


def window_block(block):
    own = lax.axis_index("edge")
    group, own_group = block // 4, own // 4
    column = ((block // 2) % 2 != (own // 2) % 2).astype(jnp.int32)
    place = jnp.where(group == own_group, 0, jnp.where(group == own_group ^ 1, 2, 4)) + column
    place = jnp.where(jnp.abs(group - own_group) == 2, 6, place)
    return place + 7 * (block % 2 != own % 2).astype(jnp.int32)


def corr_picks():
    side = 2 * CORR_X + 1
    picks = np.zeros((ROWS, PIX, (2 * CORR_Y + 1) * side), np.float32)
    for y in range(ROWS):
        for y2 in range(ROWS):
            for dx in range(-CORR_X, CORR_X + 1):
                if abs(y2 - y) <= CORR_Y:
                    lane = (y2 * WIDTH + WIDTH - 1 - dx) % PIX
                    picks[y, lane, (y2 - y + CORR_Y) * side + dx + CORR_X] = 1
    return jnp.asarray(picks, jnp.bfloat16)


def conv_inputs(pair):
    return [r for r in range(2 * pair - 1, 2 * pair + 3) if 0 <= r < ROWS]


def conv_weights(w_cand, w_motion):
    blank = jnp.zeros_like(w_motion)
    pairs = []
    for pair in range(ROWS // 2):
        rows = []
        for dx in range(3):
            for r in conv_inputs(pair):
                rows.append(
                    jnp.concatenate(
                        [
                            w_cand[3 * (r - y + 1) + dx] if abs(r - y) <= 1 else blank
                            for y in (2 * pair, 2 * pair + 1)
                        ],
                        1,
                    )
                )
        rows.append(jnp.concatenate([w_motion, blank], 1))
        rows.append(jnp.concatenate([blank, w_motion], 1))
        pairs.append(jnp.concatenate(rows, 0))
    return jnp.stack(pairs)


def edge_kernel(
    batch, index_ref, target_ref, feat_ref, ctx_ref, state_ref, window_ref, picks_ref, w_corr_ref,
    w_gates_ref, w_conv_ref, w_heads_ref, new_ref, sums_ref, held_ref, sem
):
    chans = feat_ref.shape[-1]
    edges = state_ref.shape[0]
    neigh = edges // feat_ref.shape[0]
    narrow = jnp.bfloat16
    sums_ref[...] = jnp.zeros_like(sums_ref)
    inv_root = 1.0 / math.sqrt(chans)
    xs = lax.broadcasted_iota(jnp.int32, (WIDTH, PIX), 0)
    lanes = lax.broadcasted_iota(jnp.int32, (WIDTH, PIX), 1)
    scales = []
    for k in range(SHARE):
        target = WIDTH - 1 - (lanes + PIX - k * (WIDTH // SHARE)) % WIDTH
        scales.append(jnp.where(jnp.abs(target - xs) <= CORR_X, inv_root, 0.0).astype(jnp.float32))
    w_corr = []
    for y in range(ROWS):
        base = jnp.dot(picks_ref[y], w_corr_ref[...], preferred_element_type=jnp.float32)
        base = base.astype(narrow)
        turns = [(PIX - k * (WIDTH // SHARE)) % PIX for k in range(SHARE)]
        w_corr.append(jnp.concatenate([jnp.concatenate([base[t:], base[:t]], 0) if t else base for t in turns], 1))
    w_gates = w_gates_ref[...] * jnp.bfloat16(0.5)
    heads_wide = w_heads_ref[...].astype(jnp.float32)
    blank = jnp.zeros_like(heads_wide[:1])
    w_heads = jnp.concatenate(
        [
            jnp.concatenate([heads_wide[r : r + 1] if p == j else blank for p in range(2)], 1)
            for r in range(2)
            for j in range(2)
        ],
        0,
    ).astype(narrow)
    cols = lax.broadcasted_iota(jnp.int32, (WIDTH, chans), 0)
    has_left = jnp.concatenate([cols > 0] * batch, 0)
    has_right = jnp.concatenate([cols < WIDTH - 1] * batch, 0)
    length = batch * WIDTH
    quarter = batch // SHARE
    copies = []
    for start in range(0, edges, batch):
        these = list(range(start, start + batch))
        scores = []
        for i, e in enumerate(these):
            target = window_ref.at[index_ref[e // neigh, e % neigh]]
            turn = i // quarter * (WIDTH // SHARE)
            target = [target[PIX - turn :], target[: PIX - turn]] if turn else [target[...]]
            scores.append(
                lax.dot_general(
                    feat_ref[e // neigh], jnp.concatenate(target, 0),
                    (((1,), (1,)), ((), ())), preferred_element_type=jnp.float32,
                )
            )
        motion, hidden, update_tanh, reset = [], [], [], []
        for y in range(ROWS):
            row = slice(y * WIDTH, (y + 1) * WIDTH)
            shared = []
            for i in range(quarter):
                bands = sum(scores[i + k * quarter][row] * scales[k] for k in range(SHARE))
                shared.append(pltpu.roll(bands, 0, 1, stride=1, stride_axis=0).astype(narrow))
            encoded = jnp.dot(
                jnp.concatenate(shared, 0), w_corr[y], preferred_element_type=jnp.float32
            )
            encoded = jnp.concatenate(
                [encoded[:, k * chans : (k + 1) * chans] for k in range(SHARE)], 0
            )
            ctx = jnp.concatenate([ctx_ref[e // neigh, row] for e in these], 0)
            motion.append((jnp.maximum(encoded, 0.0) + ctx.astype(jnp.float32)).astype(narrow))
            hidden.append(jnp.concatenate([state_ref[e, row] for e in these], 0))
        for y in range(ROWS):
            gates = jnp.tanh(
                jnp.dot(
                    jnp.concatenate([hidden[y], motion[y]], 1), w_gates,
                    preferred_element_type=jnp.float32,
                )
            )
            half_hidden = 0.5 * hidden[y].astype(jnp.float32)
            update_tanh.append(gates[:, :chans])
            reset.append(half_hidden + half_hidden * gates[:, chans:])
        left = [jnp.where(has_left, pltpu.roll(r, 1, 0), 0.0).astype(narrow) for r in reset]
        right = [
            jnp.where(has_right, pltpu.roll(r, length - 1, 0), 0.0).astype(narrow) for r in reset
        ]
        centre = [r.astype(narrow) for r in reset]
        done = []
        for pair in range(ROWS // 2):
            taps = [side[r] for side in (left, centre, right) for r in conv_inputs(pair)]
            taps = jnp.concatenate(taps + motion[2 * pair : 2 * pair + 2], 1)
            conv = jnp.dot(taps, w_conv_ref[pair], preferred_element_type=jnp.float32)
            for part in range(2):
                y = 2 * pair + part
                wide = hidden[y].astype(jnp.float32)
                update = 0.5 + 0.5 * update_tanh[y]
                candidate = jnp.tanh(conv[:, part * chans : (part + 1) * chans])
                done.append((wide + update * (candidate - wide)).astype(narrow))
                for i, e in enumerate(these):
                    held_ref[e, y * WIDTH : (y + 1) * WIDTH] = done[y][i * WIDTH : (i + 1) * WIDTH]
            place = (pl.ds(start, batch), pl.ds(2 * pair * WIDTH, 2 * WIDTH))
            copies.append(
                pltpu.make_async_copy(
                    held_ref.at[place], new_ref.at[place], sem.at[start // batch, pair]
                )
            )
            copies[-1].start()
        for i in range(0, batch, 2):
            mine = [
                jnp.concatenate([n[j * WIDTH : (j + 1) * WIDTH] for n in done], 0)
                for j in (i, i + 1)
            ]
            heads = lax.dot_general(
                w_heads, jnp.concatenate(mine, 1), (((1,), (1,)), ((), ())),
                preferred_element_type=jnp.float32,
            )
            confidence = 0.5 + 0.5 * jnp.tanh(0.5 * heads[2:4])
            pushed = confidence * heads[0:2]
            for j in range(2):
                e = start + i + j
                sums_ref[target_ref[e // neigh, e % neigh]] += jnp.concatenate(
                    [pushed[j : j + 1], confidence[j : j + 1]], 0
                )
    for copy in copies:
        copy.wait()


def on_device(
    features, context, states, neighbours, depths, damping,
    w_corr, w_gates, w_cand, w_motion, w_heads,
):
    frames_here, pixels, chans = features.shape
    edges = frames_here * states.shape[1]
    mirrored = features.reshape(frames_here, ROWS, WIDTH, chans)[:, :, ::-1].reshape(features.shape)
    window = jnp.concatenate(gather_window(mirrored), 0)
    blocks = neighbours // frames_here
    local_index = window_block(blocks) * frames_here + neighbours % frames_here
    frames_all = lax.axis_size("edge") * frames_here
    batch = 12
    vmem = pl.BlockSpec(memory_space=pltpu.VMEM)
    smem = pl.BlockSpec(memory_space=pltpu.SMEM)
    new_states, sums = pl.pallas_call(
        functools.partial(edge_kernel, batch),
        out_shape=(
            jax.ShapeDtypeStruct((edges, pixels, chans), states.dtype),
            jax.ShapeDtypeStruct((frames_all, 2, pixels), jnp.float32),
        ),
        in_specs=[smem, smem] + [vmem] * 9,
        out_specs=[pl.BlockSpec(memory_space=pl.ANY), vmem],
        scratch_shapes=[
            pltpu.VMEM((edges, pixels, chans), states.dtype),
            pltpu.SemaphoreType.DMA((edges // batch, ROWS // 2)),
        ],
        compiler_params=pltpu.CompilerParams(vmem_limit_bytes=32 * 1024 * 1024),
        name="edge_update",
    )(
        local_index, neighbours, features, context, states.reshape(edges, pixels, chans),
        window, corr_picks(), w_corr, w_gates,
        conv_weights(w_cand, w_motion), w_heads,
    )
    new_states = new_states.reshape(states.shape)
    sums = sums.reshape(-1, frames_here, 2, pixels)
    sums = jnp.sum(lax.all_to_all(sums, "edge", 0, 0, tiled=True), 0)
    new_depths = depths + sums[:, 0] / (damping + sums[:, 1])
    return (new_states, new_depths)


def solution(mesh):
    split = P(("groups", "edge"))
    return jax.shard_map(
        on_device,
        mesh=mesh,
        in_specs=(split,) * 6 + (P(),) * 5,
        out_specs=(split, split),
        check_vma=False,
    )
```

```python
import functools
import math

import jax
import jax.numpy as jnp
import numpy as np
from jax import lax
from jax.experimental import pallas as pl
from jax.experimental.pallas import tpu as pltpu
from jax.sharding import PartitionSpec as P

REACH = 6
CORR_X = 3
CORR_Y = 3
WIDTH = 64
ROWS = 4
SHARE = 4
PIX = ROWS * WIDTH


def sent(value, pairs):
    count = lax.axis_size("edge")
    return lax.ppermute(
        value, "edge", [(a, b) for a, b in pairs if 0 <= a < count and 0 <= b < count]
    )


def swapped(value, steps, odd):
    low = [i for i in range(lax.axis_size("edge")) if (i // steps) % 2 == odd]
    low = [i for i in low if i + steps < lax.axis_size("edge")]
    return sent(value, [(i, i + steps) for i in low] + [(i + steps, i) for i in low])


def gather_window(own):
    count = lax.axis_size("edge")
    beside = swapped(own, 2, 0)
    two = jnp.concatenate([own, beside], 0)
    step = [REACH, 8]
    far = sent(own, [(i, i + step[i % 2] * (1 if i % 4 >= 2 else -1)) for i in range(count)])
    far = sent(far, [(i, i ^ 2 if i % 2 else i) for i in range(count)])
    even = swapped(two, 4, 0)
    odd = swapped(two, 4, 1)
    mine = [two, even, odd, far]
    return mine + [swapped(piece, 1, 0) for piece in mine]


def window_block(block):
    own = lax.axis_index("edge")
    group, own_group = block // 4, own // 4
    column = ((block // 2) % 2 != (own // 2) % 2).astype(jnp.int32)
    place = jnp.where(group == own_group, 0, jnp.where(group == own_group ^ 1, 2, 4)) + column
    place = jnp.where(jnp.abs(group - own_group) == 2, 6, place)
    return place + 7 * (block % 2 != own % 2).astype(jnp.int32)


def corr_picks():
    side = 2 * CORR_X + 1
    picks = np.zeros((ROWS, PIX, (2 * CORR_Y + 1) * side), np.float32)
    for y in range(ROWS):
        for y2 in range(ROWS):
            for dx in range(-CORR_X, CORR_X + 1):
                if abs(y2 - y) <= CORR_Y:
                    lane = (y2 * WIDTH + WIDTH - 1 - dx) % PIX
                    picks[y, lane, (y2 - y + CORR_Y) * side + dx + CORR_X] = 1
    return jnp.asarray(picks, jnp.bfloat16)


def conv_inputs(pair):
    return [r for r in range(2 * pair - 1, 2 * pair + 3) if 0 <= r < ROWS]


def conv_weights(w_cand, w_motion):
    blank = jnp.zeros_like(w_motion)
    pairs = []
    for pair in range(ROWS // 2):
        rows = []
        for dx in range(3):
            for r in conv_inputs(pair):
                rows.append(
                    jnp.concatenate(
                        [
                            w_cand[3 * (r - y + 1) + dx] if abs(r - y) <= 1 else blank
                            for y in (2 * pair, 2 * pair + 1)
                        ],
                        1,
                    )
                )
        rows.append(jnp.concatenate([w_motion, blank], 1))
        rows.append(jnp.concatenate([blank, w_motion], 1))
        pairs.append(jnp.concatenate(rows, 0))
    return jnp.stack(pairs)


def edge_kernel(
    batch, index_ref, target_ref, feat_ref, ctx_ref, state_ref, window_ref, picks_ref, w_corr_ref,
    w_gates_ref, w_conv_ref, w_heads_ref, new_ref, sums_ref, held_ref, sem
):
    chans = feat_ref.shape[-1]
    edges = state_ref.shape[0]
    neigh = edges // feat_ref.shape[0]
    narrow = jnp.bfloat16
    sums_ref[...] = jnp.zeros_like(sums_ref)
    inv_root = 1.0 / math.sqrt(chans)
    xs = lax.broadcasted_iota(jnp.int32, (WIDTH, PIX), 0)
    lanes = lax.broadcasted_iota(jnp.int32, (WIDTH, PIX), 1)
    scales = []
    for k in range(SHARE):
        target = WIDTH - 1 - (lanes + PIX - k * (WIDTH // SHARE)) % WIDTH
        scales.append(jnp.where(jnp.abs(target - xs) <= CORR_X, inv_root, 0.0).astype(jnp.float32))
    w_corr = []
    for y in range(ROWS):
        base = jnp.dot(picks_ref[y], w_corr_ref[...], preferred_element_type=jnp.float32)
        base = base.astype(narrow)
        turns = [(PIX - k * (WIDTH // SHARE)) % PIX for k in range(SHARE)]
        w_corr.append(jnp.concatenate([jnp.concatenate([base[t:], base[:t]], 0) if t else base for t in turns], 1))
    w_gates = w_gates_ref[...] * jnp.bfloat16(0.5)
    heads_wide = w_heads_ref[...].astype(jnp.float32)
    blank = jnp.zeros_like(heads_wide[:1])
    w_heads = jnp.concatenate(
        [
            jnp.concatenate([heads_wide[r : r + 1] if p == j else blank for p in range(2)], 1)
            for r in range(2)
            for j in range(2)
        ],
        0,
    ).astype(narrow)
    cols = lax.broadcasted_iota(jnp.int32, (WIDTH, chans), 0)
    has_left = jnp.concatenate([cols > 0] * batch, 0)
    has_right = jnp.concatenate([cols < WIDTH - 1] * batch, 0)
    length = batch * WIDTH
    quarter = batch // SHARE
    copies = []
    finished = []
    all_scores = {}
    for start in range(0, edges, batch):
        these = list(range(start, start + batch))
        scores = []
        for i, e in enumerate(these):
            target = window_ref.at[index_ref[e // neigh, e % neigh]]
            turn = i // quarter * (WIDTH // SHARE)
            target = [target[PIX - turn :], target[: PIX - turn]] if turn else [target[...]]
            scores.append(
                lax.dot_general(
                    feat_ref[e // neigh], jnp.concatenate(target, 0),
                    (((1,), (1,)), ((), ())), preferred_element_type=jnp.float32,
                )
            )
        all_scores[start] = scores
    for start in range(0, edges, batch):
        these = list(range(start, start + batch))
        scores = all_scores[start]
        motion, hidden, update_tanh, reset = [], [], [], []
        for y in range(ROWS):
            row = slice(y * WIDTH, (y + 1) * WIDTH)
            shared = []
            for i in range(quarter):
                bands = sum(scores[i + k * quarter][row] * scales[k] for k in range(SHARE))
                shared.append(pltpu.roll(bands, 0, 1, stride=1, stride_axis=0).astype(narrow))
            encoded = jnp.dot(
                jnp.concatenate(shared, 0), w_corr[y], preferred_element_type=jnp.float32
            )
            encoded = jnp.concatenate(
                [encoded[:, k * chans : (k + 1) * chans] for k in range(SHARE)], 0
            )
            ctx = jnp.concatenate([ctx_ref[e // neigh, row] for e in these], 0)
            motion.append((jnp.maximum(encoded, 0.0) + ctx.astype(jnp.float32)).astype(narrow))
            hidden.append(jnp.concatenate([state_ref[e, row] for e in these], 0))
        for y in range(ROWS):
            gates = jnp.tanh(
                jnp.dot(
                    jnp.concatenate([hidden[y], motion[y]], 1), w_gates,
                    preferred_element_type=jnp.float32,
                )
            )
            half_hidden = 0.5 * hidden[y].astype(jnp.float32)
            update_tanh.append(gates[:, :chans])
            reset.append(half_hidden + half_hidden * gates[:, chans:])
        left = [jnp.where(has_left, pltpu.roll(r, 1, 0), 0.0).astype(narrow) for r in reset]
        right = [
            jnp.where(has_right, pltpu.roll(r, length - 1, 0), 0.0).astype(narrow) for r in reset
        ]
        centre = [r.astype(narrow) for r in reset]
        done = []
        for pair in range(ROWS // 2):
            taps = [side[r] for side in (left, centre, right) for r in conv_inputs(pair)]
            taps = jnp.concatenate(taps + motion[2 * pair : 2 * pair + 2], 1)
            conv = jnp.dot(taps, w_conv_ref[pair], preferred_element_type=jnp.float32)
            for part in range(2):
                y = 2 * pair + part
                wide = hidden[y].astype(jnp.float32)
                update = 0.5 + 0.5 * update_tanh[y]
                candidate = jnp.tanh(conv[:, part * chans : (part + 1) * chans])
                done.append((wide + update * (candidate - wide)).astype(narrow))
                for i, e in enumerate(these):
                    held_ref[e, y * WIDTH : (y + 1) * WIDTH] = done[y][i * WIDTH : (i + 1) * WIDTH]
            place = (pl.ds(start, batch), pl.ds(2 * pair * WIDTH, 2 * WIDTH))
            copies.append(
                pltpu.make_async_copy(
                    held_ref.at[place], new_ref.at[place], sem.at[start // batch, pair]
                )
            )
            copies[-1].start()
        finished.append((start, done))
    for start, done in finished:
        for i in range(0, batch, 2):
            mine = [
                jnp.concatenate([n[j * WIDTH : (j + 1) * WIDTH] for n in done], 0)
                for j in (i, i + 1)
            ]
            heads = lax.dot_general(
                w_heads, jnp.concatenate(mine, 1), (((1,), (1,)), ((), ())),
                preferred_element_type=jnp.float32,
            )
            confidence = 0.5 + 0.5 * jnp.tanh(0.5 * heads[2:4])
            pushed = confidence * heads[0:2]
            for j in range(2):
                e = start + i + j
                sums_ref[target_ref[e // neigh, e % neigh]] += jnp.concatenate(
                    [pushed[j : j + 1], confidence[j : j + 1]], 0
                )
    for copy in copies:
        copy.wait()


def on_device(
    features, context, states, neighbours, depths, damping,
    w_corr, w_gates, w_cand, w_motion, w_heads,
):
    frames_here, pixels, chans = features.shape
    edges = frames_here * states.shape[1]
    mirrored = features.reshape(frames_here, ROWS, WIDTH, chans)[:, :, ::-1].reshape(features.shape)
    window = jnp.concatenate(gather_window(mirrored), 0)
    blocks = neighbours // frames_here
    local_index = window_block(blocks) * frames_here + neighbours % frames_here
    frames_all = lax.axis_size("edge") * frames_here
    batch = 12
    vmem = pl.BlockSpec(memory_space=pltpu.VMEM)
    smem = pl.BlockSpec(memory_space=pltpu.SMEM)
    new_states, sums = pl.pallas_call(
        functools.partial(edge_kernel, batch),
        out_shape=(
            jax.ShapeDtypeStruct((edges, pixels, chans), states.dtype),
            jax.ShapeDtypeStruct((frames_all, 2, pixels), jnp.float32),
        ),
        in_specs=[smem, smem] + [vmem] * 9,
        out_specs=[pl.BlockSpec(memory_space=pl.ANY), vmem],
        scratch_shapes=[
            pltpu.VMEM((edges, pixels, chans), states.dtype),
            pltpu.SemaphoreType.DMA((edges // batch, ROWS // 2)),
        ],
        compiler_params=pltpu.CompilerParams(vmem_limit_bytes=32 * 1024 * 1024),
        name="edge_update",
    )(
        local_index, neighbours, features, context, states.reshape(edges, pixels, chans),
        window, corr_picks(), w_corr, w_gates,
        conv_weights(w_cand, w_motion), w_heads,
    )
    new_states = new_states.reshape(states.shape)
    sums = sums.reshape(-1, frames_here, 2, pixels)
    sums = jnp.sum(lax.all_to_all(sums, "edge", 0, 0, tiled=True), 0)
    new_depths = depths + sums[:, 0] / (damping + sums[:, 1])
    return (new_states, new_depths)


def solution(mesh):
    split = P(("groups", "edge"))
    return jax.shard_map(
        on_device,
        mesh=mesh,
        in_specs=(split,) * 6 + (P(),) * 5,
        out_specs=(split, split),
        check_vma=False,
    )
```
